512 devices in a mesh: span: 16 (over x, z_hi, core), seq: 32 (over z_lo, y).
Axes of the slice: x: 4, y: 8, z: 8 (z_hi: 2, z_lo: 4; z = z_hi * 4 + z_lo), core: 2. Of those that a mesh axis runs over, the one named last changes fastest.
Arguments:
- queries: bfloat16 [16, 768, 4096], P('span', 'seq'), may hold values from -160 to 160
- keys: bfloat16 [16, 768, 4096], P('span', 'seq'), may hold values from -5 to 5
- values: bfloat16 [16, 768, 4096], P('span', 'seq'), may hold values from -6 to 6
- step_index: int32 [16], replicated, may hold values from 0 to 15
- frame_counts: int32 [16], replicated, may hold values from 1 to 8
- frame_layout: int32 [8, 8], replicated, may hold values 0 or 1
- gate_table: float32 [16, 4096], replicated, may hold values from -8 to 8
Outputs:
- mixed: bfloat16 [16, 768, 4096], P('span', 'seq')
The draws below stay inside these ranges and needn't reach their ends.
All inputs are finite; a program needn't handle non-finite values.
Results may differ from the reference program's by a relative error of at most 0.0075.
Values may be sent and summed in bfloat16 or wider, within the bound.
A program may use at most 64 MiB of HBM per device.

```python
import math
import jax
import jax.numpy as jnp
from jax import lax

HD = 128
FRAMES = 8
STEPS = 16
HEADS = 32
SPANS = 16
CTOK = 768


def shared_keys(key):
    return jnp.clip(jax.random.normal(key, (SPANS, CTOK, HEADS * HD), jnp.float32), -5.0, 5.0)


def draw_keys(key, part):
    base_keys = shared_keys(key)
    return base_keys.astype(jnp.bfloat16)


def draw_queries(key, part):
    key = jax.random.fold_in(key, 13)
    fresh = 2.0 * jnp.clip(jax.random.normal(key, (SPANS, CTOK, HEADS * HD), jnp.float32), -5.0, 5.0)
    return fresh.astype(jnp.bfloat16)


def place_ends(result, rng, smallest, high):
    shape = result.shape
    index_at = [jax.random.randint(jax.random.fold_in(rng, axis), (), 0, shape[axis]) for axis in range(len(shape))]
    result = result.at[tuple(index_at)].set(smallest)
    longest = shape.index(max(shape))
    index_at[longest] = (index_at[longest] + 1) % shape[longest]
    return result.at[tuple(index_at)].set(high)


def level_of(own_key, extent, pieces, low, largest):
    loudness, own = 1.0, jax.random.fold_in(own_key, 6)
    for dim, shards_of in pieces:
        heights = jnp.exp(jax.random.uniform(jax.random.fold_in(own, dim), (shards_of,), jnp.float32, low / len(pieces), largest / len(pieces)))
        loudness = loudness * jnp.repeat(heights, extent[dim] // shards_of).reshape([-1 if axis == dim else 1 for axis in range(len(extent))])
    return loudness


def normal_values(stream_key, dims, scale, most, split=(), dtype=jnp.bfloat16):
    array = jax.random.normal(stream_key, dims, jnp.float32) * scale
    if len(split) > 0:
        array = level_of(stream_key, dims, split, -0.22, 0.18) * array
    return jnp.clip(array, min=-most, max=most).astype(dtype)


def setup_inputs(seed: int = 0) -> dict:
    key_list = jax.random.split(jax.random.key(seed), 8)
    queries = draw_queries(jax.random.fold_in(key_list[7], 71), 0)
    keys = draw_keys(jax.random.fold_in(key_list[7], 71), 0)
    values = normal_values(key_list[2], (SPANS, CTOK, HEADS * HD), 1.0, 6.0, ((0, 16), (1, 32)))
    step_index = place_ends(jax.random.randint(key_list[3], (SPANS,), 0, STEPS), jax.random.fold_in(key_list[3], 1), 0, STEPS - 1).astype(jnp.int32)
    frame_counts = place_ends(jax.random.randint(key_list[4], (SPANS,), 1, FRAMES + 1), jax.random.fold_in(key_list[4], 1), 1, FRAMES).astype(jnp.int32)
    frame_layout = place_ends((jax.random.randint(key_list[5], (FRAMES, FRAMES), 0, 2) < 1).astype(jnp.int32), jax.random.fold_in(key_list[5], 1), 0, 1)
    gate_table = normal_values(key_list[6], (STEPS, HEADS * HD), 2.0, 8.0, (), jnp.float32)
    return {"queries": queries, "keys": keys, "values": values, "step_index": step_index, "frame_counts": frame_counts, "frame_layout": frame_layout, "gate_table": gate_table}


def reference(queries, keys, values, step_index, frame_counts, frame_layout, gate_table):
    frame_tok = CTOK // FRAMES
    score_scale = 1.0 / math.sqrt(HD)
    query_frame = jnp.arange(CTOK) // frame_tok
    results = []
    for span_pos in range(SPANS):
        key_rows = (span_pos + 1) * CTOK
        row_ids = jnp.arange(key_rows)
        key_span = row_ids // CTOK
        key_frame = row_ids % CTOK // frame_tok
        earlier = (key_span < span_pos) & (key_frame < frame_counts[key_span])
        layout_hit = frame_layout[query_frame][:, key_frame] == 1
        same_frame = query_frame[:, None] == key_frame[None, :]
        own_frames = (key_span == span_pos)[None, :] & ((key_frame < frame_counts[span_pos])[None, :] & layout_hit | same_frame)
        visible = earlier[None, :] | own_frames
        query_heads = queries[span_pos].reshape(CTOK, HEADS, HD).transpose(1, 0, 2)
        key_heads = keys[:span_pos + 1].reshape(key_rows, HEADS, HD).transpose(1, 0, 2)
        value_heads = values[:span_pos + 1].reshape(key_rows, HEADS, HD).transpose(1, 0, 2)

        def one_head(operands):
            query_one, key_one, value_one = operands
            scores = jnp.dot(query_one, key_one.T, preferred_element_type=jnp.float32) * score_scale
            masked = jnp.where(visible, scores, -1e+30)
            row_max = lax.optimization_barrier(jnp.max(masked, axis=1, keepdims=True))
            exps = jnp.where(visible, jnp.exp(masked - row_max), 0.0)
            totals = lax.optimization_barrier(jnp.sum(exps, axis=1, keepdims=True))
            weights = exps.astype(jnp.bfloat16)
            summed = jnp.dot(weights, value_one, preferred_element_type=jnp.float32)
            return (summed / totals).astype(jnp.bfloat16)
        attended = lax.map(one_head, (query_heads, key_heads, value_heads))
        attended = attended.transpose(1, 0, 2).reshape(CTOK, HEADS * HD)
        gate_row = gate_table[step_index[span_pos]]
        results.append((attended.astype(jnp.float32) * gate_row[None, :]).astype(jnp.bfloat16))
    return jnp.stack(results)
```

```python
import functools
import math

import jax
import jax.numpy as jnp
from jax import lax
from jax.experimental import pallas as pl
from jax.experimental.pallas import tpu as pltpu
from jax.sharding import PartitionSpec as P

MESH = pl.DeviceIdType.MESH
HD = 128
FRAMES = 8
SPANS = 16
ROWS = 768
PIECE = 24
PEERS = 32
FRAME_ROWS = ROWS // FRAMES
SCALE = math.log2(math.e) / math.sqrt(HD)
LOW = -1e30
F32, BF16 = jnp.float32, jnp.bfloat16


def whole(ref, sem):
    return pltpu.make_async_copy(ref, ref, sem)


def kernel(
    q_ref, k_ref, v_ref, step_ref, count_ref, layout_ref, gate_ref, out_ref,
    kg, vg, qg, kx, vt, qt, s_buf, m_buf, acc, obuf, part_out, stat_out, part_in, stat_in,
    a2a_send, a2a_recv, ring_send, ring_recv, pair_send, pair_recv,
):
    span = lax.axis_index("span")
    seq = lax.axis_index("seq")
    core = lax.rem(span, 2)
    z_hi = lax.rem(lax.div(span, 2), 2)
    x = lax.div(span, 4)
    z_lo = lax.div(seq, 8)
    y = lax.rem(seq, 8)
    half = lax.rem(z_lo, 2)
    plane = z_hi * 2 + lax.div(z_lo, 2)
    head = plane * 8 + y
    role = (x * 2 + half) * 2 + core
    own = x * 2 + core
    has_self = (half == z_hi).astype(jnp.int32)

    def ring_span(pos):
        return (pos * 2 + z_hi) * 2 + core

    right_x, left_x, far_x = lax.rem(x + 1, 4), lax.rem(x + 3, 4), lax.rem(x + 2, 4)
    right = (ring_span(right_x), seq)
    left = (ring_span(left_x), seq)
    sibling = (span + 1 - 2 * core, seq)
    partner = (span, seq + 8 - 16 * half)

    barrier = pltpu.get_barrier_semaphore()

    def source_of(turn):
        return lax.rem(z_lo + lax.div(turn, 8), 4) * 8 + lax.rem(y + lax.rem(turn, 8), 8)

    def greet(turn, carry):
        pl.semaphore_signal(barrier, inc=1, device_id=(role, source_of(turn)), device_id_type=MESH)
        return carry

    lax.fori_loop(1, PEERS, greet, 0)

    @pl.when(has_self == 0)
    def _():
        greet(0, 0)

    for other in (right, left, sibling, partner):
        pl.semaphore_signal(barrier, inc=1, device_id=other, device_id_type=MESH)
    pl.semaphore_wait(barrier, PEERS + 4 - has_self)

    def scatter(array_ref, landing, which):
        def target(turn):
            to_plane = lax.rem(plane + lax.div(turn, 8), 4)
            to_y = lax.rem(y + lax.rem(turn, 8), 8)
            to_span = (x * 2 + lax.div(to_plane, 2)) * 2 + core
            to_seq = (2 * lax.rem(to_plane, 2) + z_hi) * 8 + to_y
            columns = pl.ds(pl.multiple_of((to_plane * 8 + to_y) * HD, HD), HD)
            return (to_span, to_seq), array_ref.at[:, columns], landing.at[seq]

        def send(turn, carry):
            device, source, destination = target(turn)
            pltpu.make_async_remote_copy(
                src_ref=source, dst_ref=destination, send_sem=a2a_send.at[which],
                recv_sem=a2a_recv.at[which], device_id=device, device_id_type=MESH,
            ).start()
            return carry

        @pl.when(has_self == 1)
        def _():
            _, source, destination = target(0)
            pltpu.make_async_copy(source, destination, a2a_recv.at[which]).start()

        @pl.when(has_self == 0)
        def _():
            send(0, 0)

        lax.fori_loop(1, PEERS, send, 0)

    scatter(k_ref, kg.at[own], 1)
    scatter(q_ref, qg.at[0], 0)
    scatter(v_ref, vg.at[own], 2)

    rows = lax.broadcasted_iota(jnp.int32, (ROWS, HD), 0)
    cols = lax.broadcasted_iota(jnp.int32, (ROWS, HD), 1)
    for item in range(8):
        count = count_ref[(item // 2) * 4 + half * 2 + item % 2]
        hidden = (cols == FRAMES) & (rows >= count * FRAME_ROWS)
        kx[item, :, HD:] = jnp.where(hidden, LOW, 0.0).astype(BF16)
        vt[item, HD:, :] = jnp.ones((16, ROWS), BF16)
    first = cols * FRAME_ROWS
    kx[own, :, HD:] = ((cols < FRAMES) & (rows >= first) & (rows < first + FRAME_ROWS)).astype(F32).astype(BF16)
    frame_id = lax.broadcasted_iota(jnp.int32, (16, ROWS), 0)
    lane = lax.broadcasted_iota(jnp.int32, (16, ROWS), 1)
    own_count = count_ref[role]
    hit = jnp.zeros((16, ROWS), jnp.int32)
    for q_frame in range(FRAMES):
        column = jnp.zeros((16, ROWS), jnp.int32)
        for k_frame in range(FRAMES):
            column = jnp.where(frame_id == k_frame, layout_ref[q_frame, k_frame], column)
        inside = (lane >= q_frame * FRAME_ROWS) & (lane < (q_frame + 1) * FRAME_ROWS)
        hit = jnp.where(inside, column, hit)
    valid = frame_id < own_count
    same = (lane >= frame_id * FRAME_ROWS) & (lane < (frame_id + 1) * FRAME_ROWS)
    shown = (valid & (hit == 1)) | same
    one_row = jnp.where(frame_id == FRAMES, 1.0, 0.0)
    in_frames = frame_id < FRAMES
    qt[0, HD:HD + 16, :] = jnp.where(in_frames & jnp.logical_not(shown), LOW, one_row).astype(BF16)
    qt[1, HD:HD + 16, :] = jnp.where(in_frames & jnp.logical_not(valid), LOW, one_row).astype(BF16)
    qt[:, HD + 16:, :] = jnp.zeros((2, HD - 16, ROWS), BF16)
    m_buf[...] = jnp.full_like(m_buf, LOW)
    acc[...] = jnp.zeros_like(acc)

    gathered = (kg, vg)

    def hop(array, number, item, device, rows_from=0, row_count=PEERS):
        piece = gathered[array].at[item, pl.ds(rows_from, row_count)]
        return pltpu.make_async_remote_copy(
            src_ref=piece, dst_ref=piece, send_sem=ring_send.at[array, number],
            recv_sem=ring_recv.at[array, number], device_id=device, device_id_type=MESH,
        )

    other_core = 1 - core
    left_item, right_item, far_item = left_x * 2 + core, right_x * 2 + core, far_x * 2 + core
    near_half, back_half = PEERS // 2, PEERS // 2

    def outgoing(array):
        return (
            hop(array, 0, own, right),
            hop(array, 1, own, left),
            hop(array, 2, own, sibling),
            hop(array, 3, left_item, right, 0, near_half),
            hop(array, 4, right_item, left, near_half, back_half),
            hop(array, 5, left_item, sibling),
            hop(array, 6, right_item, sibling),
            hop(array, 7, far_item, sibling, 0, near_half),
            hop(array, 8, far_item, sibling, near_half, back_half),
        )

    def incoming(array):
        return (
            hop(array, 0, left_item, right),
            hop(array, 1, right_item, left),
            hop(array, 2, x * 2 + other_core, sibling),
            hop(array, 3, far_item, right, 0, near_half),
            hop(array, 4, far_item, left, near_half, back_half),
            hop(array, 5, left_x * 2 + other_core, sibling),
            hop(array, 6, right_x * 2 + other_core, sibling),
            hop(array, 7, far_x * 2 + other_core, sibling, 0, near_half),
            hop(array, 8, far_x * 2 + other_core, sibling, near_half, back_half),
        )

    k_out, v_out, k_in, v_in = outgoing(0), outgoing(1), incoming(0), incoming(1)

    def flat(piece):
        return piece.astype(F32).reshape(ROWS, HD).astype(BF16)

    def take_keys(item):
        kx[item, :, :HD] = flat(kg[item])

    def take_values(item):
        vt[item, :HD, :] = flat(vg[item]).T

    def scores(slot, item, side):
        result = jnp.dot(kx[item], qt[side], preferred_element_type=F32)
        s_buf[slot] = result
        return jnp.max(result, axis=0, keepdims=True)

    def absorb(slot, item, side, block_max):
        old_max = m_buf[side]
        new_max = jnp.maximum(old_max, block_max)
        weights = jnp.exp2(s_buf[slot] * SCALE - new_max * SCALE).astype(BF16)
        summed = jnp.dot(vt[item], weights, preferred_element_type=F32)
        acc[side] = acc[side] * jnp.exp2((old_max - new_max) * SCALE) + summed
        m_buf[side] = new_max

    def attend(blocks):
        block_max = scores(0, *blocks[0])
        for number, block in enumerate(blocks):
            if number + 1 < len(blocks):
                next_max = scores((number + 1) % 2, *blocks[number + 1])
            absorb(number % 2, *block, block_max)
            if number + 1 < len(blocks):
                block_max = next_max

    def pair(ref_out, ref_in, number):
        return pltpu.make_async_remote_copy(
            src_ref=ref_out, dst_ref=ref_in, send_sem=pair_send.at[number],
            recv_sem=pair_recv.at[number], device_id=partner, device_id_type=MESH,
        )

    swap_queries = pair(qg.at[0], qg.at[1], 0)
    swap_part = pair(part_out, part_in, 1)
    swap_stat = pair(stat_out, stat_in, 2)

    whole(kg.at[own], a2a_recv.at[1]).wait()
    for number in range(3):
        k_out[number].start()
    take_keys(own)
    whole(qg.at[0], a2a_recv.at[0]).wait()
    swap_queries.start()
    qt[0, :HD, :] = flat(qg[0]).T
    whole(vg.at[own], a2a_recv.at[2]).wait()
    for number in range(3):
        v_out[number].start()
    take_values(own)
    attend([(own, 0)])

    for number in (0, 1):
        k_in[number].wait_recv()
    for number in (3, 4, 5, 6):
        k_out[number].start()
    sib = x * 2 + other_core
    k_in[2].wait_recv()
    v_in[2].wait_recv()
    take_keys(sib)
    take_values(sib)
    swap_queries.wait_recv()
    qt[1, :HD, :] = flat(qg[1]).T

    @pl.when(core == 1)
    def _():
        attend([(sib, 0)])

    @pl.when(half == 0)
    def _():
        attend([(own, 1), (sib, 1)])

    for number in (0, 1):
        v_in[number].wait_recv()
    for number in (3, 4, 5, 6):
        v_out[number].start()
    for array in (k_in, v_in):
        for number in (5, 6):
            array[number].wait_recv()

    def column(pos):
        mine, other = pos * 2 + core, pos * 2 + other_core
        for item in (mine, other):
            take_keys(item)
            take_values(item)
        attend([(mine, 1), (other, 1), (mine, 0), (other, 0)])

    @pl.when(x >= 1)
    def _():
        column(left_x)

    for number in (3, 4):
        k_in[number].wait_recv()
    for number in (7, 8):
        k_out[number].start()

    @pl.when(x == 3)
    def _():
        column(right_x)

    for number in (3, 4):
        v_in[number].wait_recv()
    for number in (7, 8):
        v_out[number].start()
    for array in (k_in, v_in):
        for number in (7, 8):
            array[number].wait_recv()

    @pl.when(x >= 2)
    def _():
        column(far_x)

    total = acc[1, HD:HD + 1, :]
    part_out[...] = (acc[1, :HD, :] / jnp.where(total > 0.0, total, 1.0)).astype(BF16)
    stat_out[0:1, :] = m_buf[1]
    stat_out[1:2, :] = total
    stat_out[2:, :] = jnp.zeros((6, ROWS), F32)
    swap_part.start()
    swap_stat.start()
    swap_stat.wait_recv()
    swap_part.wait_recv()
    other_max, other_total = stat_in[0:1, :], stat_in[1:2, :]
    own_max, own_total = m_buf[0], acc[0, HD:HD + 1, :]
    top = jnp.maximum(own_max, other_max)
    own_scale = jnp.exp2((own_max - top) * SCALE)
    other_weight = other_total * jnp.exp2((other_max - top) * SCALE)
    denominator = own_total * own_scale + other_weight
    mixed = (acc[0, :HD, :] * own_scale + part_in[...].astype(F32) * other_weight) / denominator
    gates = gate_ref[:, pl.ds(pl.multiple_of(head * HD, HD), HD)]
    step_id = lax.broadcasted_iota(jnp.int32, gates.shape, 0)
    gate = jnp.sum(jnp.where(step_id == step_ref[role], gates, 0.0), axis=0, keepdims=True)
    attended = mixed.T.astype(BF16).astype(F32) * gate
    obuf[...] = attended.reshape(PEERS, PIECE, HD).astype(BF16)

    columns = pl.ds(pl.multiple_of(head * HD, HD), HD)

    def give(turn, carry):
        to_seq = source_of(turn)
        pltpu.make_async_remote_copy(
            src_ref=obuf.at[to_seq], dst_ref=out_ref.at[:, columns], send_sem=a2a_send.at[3],
            recv_sem=a2a_recv.at[3], device_id=(role, to_seq), device_id_type=MESH,
        ).start()
        return carry

    @pl.when(has_self == 1)
    def _():
        pltpu.make_async_copy(obuf.at[seq], out_ref.at[:, columns], a2a_recv.at[3]).start()

    @pl.when(has_self == 0)
    def _():
        give(0, 0)

    lax.fori_loop(1, PEERS, give, 0)

    for array in (k_out, v_out):
        for copy in array:
            copy.wait_send()
    for copy in (swap_queries, swap_part, swap_stat):
        copy.wait_send()
    whole(out_ref, a2a_recv.at[3]).wait()

    @pl.when(has_self == 1)
    def _():
        for which in range(4):
            whole(obuf.at[pl.ds(0, PEERS - 1)], a2a_send.at[which]).wait()

    @pl.when(has_self == 0)
    def _():
        for which in range(4):
            whole(obuf, a2a_send.at[which]).wait()


def shards(queries, keys, values, step_index, frame_counts, frame_layout, gate_table):
    vmem = pl.BlockSpec(memory_space=pltpu.VMEM)
    smem = pl.BlockSpec(memory_space=pltpu.SMEM)
    piece = (PEERS, PIECE, HD)
    result = pl.pallas_call(
        kernel,
        out_shape=jax.ShapeDtypeStruct(queries.shape[1:], BF16),
        in_specs=[vmem, vmem, vmem, smem, smem, smem, vmem],
        out_specs=vmem,
        scratch_shapes=[
            pltpu.VMEM((8, *piece), BF16),
            pltpu.VMEM((8, *piece), BF16),
            pltpu.VMEM((2, *piece), BF16),
            pltpu.VMEM((8, ROWS, 2 * HD), BF16),
            pltpu.VMEM((8, HD + 16, ROWS), BF16),
            pltpu.VMEM((2, 2 * HD, ROWS), BF16),
            pltpu.VMEM((2, ROWS, ROWS), F32),
            pltpu.VMEM((2, 1, ROWS), F32),
            pltpu.VMEM((2, HD + 16, ROWS), F32),
            pltpu.VMEM(piece, BF16),
            pltpu.VMEM((HD, ROWS), BF16),
            pltpu.VMEM((8, ROWS), F32),
            pltpu.VMEM((HD, ROWS), BF16),
            pltpu.VMEM((8, ROWS), F32),
            pltpu.SemaphoreType.DMA((4,)),
            pltpu.SemaphoreType.DMA((4,)),
            pltpu.SemaphoreType.DMA((2, 9)),
            pltpu.SemaphoreType.DMA((2, 9)),
            pltpu.SemaphoreType.DMA((3,)),
            pltpu.SemaphoreType.DMA((3,)),
        ],
        compiler_params=pltpu.CompilerParams(
            collective_id=0, has_side_effects=True, vmem_limit_bytes=48 << 20
        ),
    )(queries[0], keys[0], values[0], step_index, frame_counts, frame_layout, gate_table)
    return result[None]


def solution(mesh):
    split = P("span", "seq", None)
    return jax.shard_map(
        shards,
        mesh=mesh,
        in_specs=(split, split, split, P(), P(), P(), P()),
        out_specs=split,
        check_vma=False,
    )
```

```python
import functools
import math

import jax
import jax.numpy as jnp
from jax import lax
from jax.experimental import pallas as pl
from jax.experimental.pallas import tpu as pltpu
from jax.sharding import PartitionSpec as P

MESH = pl.DeviceIdType.MESH
HD = 128
FRAMES = 8
SPANS = 16
ROWS = 768
PIECE = 24
PEERS = 32
FRAME_ROWS = ROWS // FRAMES
SCALE = math.log2(math.e) / math.sqrt(HD)
LOW = -1e30
F32, BF16 = jnp.float32, jnp.bfloat16


def flip(plane):
    return 1 - lax.rem(lax.div(plane + 1, 2), 2)


def whole(ref, sem):
    return pltpu.make_async_copy(ref, ref, sem)


def kernel(
    q_hbm, k_hbm, v_hbm, step_hbm, count_hbm, layout_hbm, gate_hbm, out_ref,
    q_ref, k_ref, v_ref, step_ref, count_ref, layout_ref, gate_ref, load_sem, kg, vg, qg, kx, vt, qt, s_buf, m_buf, acc, obuf, part_out, stat_out, part_in, stat_in,
    a2a_send, a2a_recv, ring_send, ring_recv, pair_send, pair_recv,
):
    span = lax.axis_index("span")
    seq = lax.axis_index("seq")
    core = lax.rem(span, 2)
    z_hi = lax.rem(lax.div(span, 2), 2)
    x = lax.div(span, 4)
    z_lo = lax.div(seq, 8)
    y = lax.rem(seq, 8)
    bit = lax.rem(z_lo, 2)
    plane = z_hi * 2 + lax.div(z_lo, 2)
    half = lax.rem(bit + flip(plane), 2)
    head = plane * 8 + y
    role = (x * 2 + half) * 2 + core
    own = x * 2 + core
    has_self = (half == z_hi).astype(jnp.int32)

    def ring_span(pos):
        return (pos * 2 + z_hi) * 2 + core

    right_x, left_x, far_x = lax.rem(x + 1, 4), lax.rem(x + 3, 4), lax.rem(x + 2, 4)
    right = (ring_span(right_x), seq)
    left = (ring_span(left_x), seq)
    sibling = (span + 1 - 2 * core, seq)
    partner = (span, seq + 8 - 16 * bit)

    columns = pl.ds(pl.multiple_of(head * HD, HD), HD)
    loads = [
        pltpu.make_async_copy(source, target, load_sem.at[number])
        for number, (source, target) in enumerate((
            (k_hbm, k_ref), (v_hbm, v_ref), (q_hbm, q_ref), (count_hbm, count_ref), (layout_hbm, layout_ref),
            (step_hbm, step_ref), (gate_hbm.at[:, columns], gate_ref),
        ))
    ]
    for load in loads:
        load.start()

    barrier = pltpu.get_barrier_semaphore()

    def source_of(turn):
        return lax.rem(z_lo + lax.div(turn, 8), 4) * 8 + lax.rem(y + lax.rem(turn, 8), 8)

    def greet(turn, carry):
        pl.semaphore_signal(barrier, inc=1, device_id=(role, source_of(turn)), device_id_type=MESH)
        return carry

    lax.fori_loop(1, PEERS, greet, 0)

    @pl.when(has_self == 0)
    def _():
        greet(0, 0)

    for other in (right, left, sibling, partner):
        pl.semaphore_signal(barrier, inc=1, device_id=other, device_id_type=MESH)
    for load in loads:
        load.wait()

    def scatter(array_ref, landing, which):
        def target(turn):
            to_plane = lax.rem(plane + lax.div(turn, 8), 4)
            to_y = lax.rem(y + lax.rem(turn, 8), 8)
            to_span = (x * 2 + lax.div(to_plane, 2)) * 2 + core
            to_bit = lax.rem(flip(to_plane) + z_hi, 2)
            to_seq = (2 * lax.rem(to_plane, 2) + to_bit) * 8 + to_y
            columns = pl.ds(pl.multiple_of((to_plane * 8 + to_y) * HD, HD), HD)
            return (to_span, to_seq), array_ref.at[:, columns], landing.at[seq]

        def send(turn, carry):
            device, source, destination = target(turn)
            pltpu.make_async_remote_copy(
                src_ref=source, dst_ref=destination, send_sem=a2a_send.at[which],
                recv_sem=a2a_recv.at[which], device_id=device, device_id_type=MESH,
            ).start()
            return carry

        @pl.when(has_self == 1)
        def _():
            _, source, destination = target(0)
            pltpu.make_async_copy(source, destination, a2a_recv.at[which]).start()

        @pl.when(has_self == 0)
        def _():
            send(0, 0)

        lax.fori_loop(1, PEERS, send, 0)

    rows = lax.broadcasted_iota(jnp.int32, (ROWS, HD), 0)
    cols = lax.broadcasted_iota(jnp.int32, (ROWS, HD), 1)
    for item in range(8):
        count = count_ref[(item // 2) * 4 + half * 2 + item % 2]
        hidden = (cols == FRAMES) & (rows >= count * FRAME_ROWS)
        kx[item, :, HD:] = jnp.where(hidden, LOW, 0.0).astype(BF16)
        vt[item, HD:, :] = jnp.ones((16, ROWS), BF16)
    first = cols * FRAME_ROWS
    kx[own, :, HD:] = ((cols < FRAMES) & (rows >= first) & (rows < first + FRAME_ROWS)).astype(F32).astype(BF16)
    frame_id = lax.broadcasted_iota(jnp.int32, (16, ROWS), 0)
    lane = lax.broadcasted_iota(jnp.int32, (16, ROWS), 1)
    own_count = count_ref[role]
    hit = jnp.zeros((16, ROWS), jnp.int32)
    for q_frame in range(FRAMES):
        column = jnp.zeros((16, ROWS), jnp.int32)
        for k_frame in range(FRAMES):
            column = jnp.where(frame_id == k_frame, layout_ref[q_frame, k_frame], column)
        inside = (lane >= q_frame * FRAME_ROWS) & (lane < (q_frame + 1) * FRAME_ROWS)
        hit = jnp.where(inside, column, hit)
    valid = frame_id < own_count
    same = (lane >= frame_id * FRAME_ROWS) & (lane < (frame_id + 1) * FRAME_ROWS)
    shown = (valid & (hit == 1)) | same
    one_row = jnp.where(frame_id == FRAMES, 1.0, 0.0)
    in_frames = frame_id < FRAMES
    qt[0, HD:HD + 16, :] = jnp.where(in_frames & jnp.logical_not(shown), LOW, one_row).astype(BF16)
    qt[1, HD:HD + 16, :] = jnp.where(in_frames & jnp.logical_not(valid), LOW, one_row).astype(BF16)
    qt[:, HD + 16:, :] = jnp.zeros((2, HD - 16, ROWS), BF16)
    m_buf[...] = jnp.full_like(m_buf, LOW)
    acc[...] = jnp.zeros_like(acc)

    pl.semaphore_wait(barrier, PEERS + 4 - has_self)
    scatter(k_ref, kg.at[own], 1)
    scatter(v_ref, vg.at[own], 2)

    gathered = (kg, vg)

    def hop(array, number, item, device, rows_from=0, row_count=PEERS):
        piece = gathered[array].at[item, pl.ds(rows_from, row_count)]
        return pltpu.make_async_remote_copy(
            src_ref=piece, dst_ref=piece, send_sem=ring_send.at[array, number],
            recv_sem=ring_recv.at[array, number], device_id=device, device_id_type=MESH,
        )

    other_core = 1 - core
    left_item, right_item, far_item = left_x * 2 + core, right_x * 2 + core, far_x * 2 + core
    lower, upper = (0, PEERS // 2), (PEERS // 2, PEERS // 2)

    def outgoing(array):
        return (
            hop(array, 0, own, right, *lower),
            hop(array, 1, own, right, *upper),
            hop(array, 2, own, left, *upper),
            hop(array, 3, own, left, *lower),
            hop(array, 4, own, sibling),
            hop(array, 5, left_item, right, *lower),
            hop(array, 6, right_item, left, *upper),
            hop(array, 7, left_item, sibling),
            hop(array, 8, right_item, sibling),
            hop(array, 9, far_item, sibling, *lower),
            hop(array, 10, far_item, sibling, *upper),
        )

    def incoming(array):
        return (
            hop(array, 0, left_item, right, *lower),
            hop(array, 1, left_item, right, *upper),
            hop(array, 2, right_item, left, *upper),
            hop(array, 3, right_item, left, *lower),
            hop(array, 4, x * 2 + other_core, sibling),
            hop(array, 5, far_item, right, *lower),
            hop(array, 6, far_item, left, *upper),
            hop(array, 7, left_x * 2 + other_core, sibling),
            hop(array, 8, right_x * 2 + other_core, sibling),
            hop(array, 9, far_x * 2 + other_core, sibling, *lower),
            hop(array, 10, far_x * 2 + other_core, sibling, *upper),
        )

    k_out, v_out, k_in, v_in = outgoing(0), outgoing(1), incoming(0), incoming(1)

    def flat(piece):
        return piece.astype(F32).reshape(ROWS, HD).astype(BF16)

    def take_keys(item):
        kx[item, :, :HD] = flat(kg[item])

    def take_values(item):
        vt[item, :HD, :] = flat(vg[item]).T

    def scores(slot, item, side):
        result = jnp.dot(kx[item], qt[side], preferred_element_type=F32)
        s_buf[slot] = result
        return jnp.max(result, axis=0, keepdims=True)

    def absorb(slot, item, side, block_max):
        old_max = m_buf[side]
        new_max = jnp.maximum(old_max, block_max)
        weights = jnp.exp2(s_buf[slot] * SCALE - new_max * SCALE).astype(BF16)
        summed = jnp.dot(vt[item], weights, preferred_element_type=F32)
        acc[side] = acc[side] * jnp.exp2((old_max - new_max) * SCALE) + summed
        m_buf[side] = new_max

    def attend(blocks):
        block_max = scores(0, *blocks[0])
        for number, block in enumerate(blocks):
            if number + 1 < len(blocks):
                next_max = scores((number + 1) % 2, *blocks[number + 1])
            absorb(number % 2, *block, block_max)
            if number + 1 < len(blocks):
                block_max = next_max

    def pair(ref_out, ref_in, number):
        return pltpu.make_async_remote_copy(
            src_ref=ref_out, dst_ref=ref_in, send_sem=pair_send.at[number],
            recv_sem=pair_recv.at[number], device_id=partner, device_id_type=MESH,
        )

    swap_queries = pair(qg.at[0], qg.at[1], 0)
    swap_part = pair(part_out, part_in, 1)
    swap_stat = pair(stat_out, stat_in, 2)

    sib = x * 2 + other_core

    def begin(copies):
        for number in (0, 2, 1, 3, 4):
            copies[number].start()

    def relay(arriving, leaving):
        arriving[0].wait_recv()
        leaving[5].start()
        arriving[2].wait_recv()
        leaving[6].start()
        arriving[1].wait_recv()
        leaving[7].start()
        arriving[3].wait_recv()
        leaving[8].start()

    def finish(arriving, leaving):
        for number in (5, 6):
            arriving[number].wait_recv()
            leaving[number + 4].start()

    whole(kg.at[own], a2a_recv.at[1]).wait()
    begin(k_out)
    scatter(q_ref, qg.at[0], 0)
    take_keys(own)
    whole(vg.at[own], a2a_recv.at[2]).wait()
    begin(v_out)
    take_values(own)
    relay(k_in, k_out)
    whole(qg.at[0], a2a_recv.at[0]).wait()
    swap_queries.start()
    qt[0, :HD, :] = flat(qg[0]).T
    relay(v_in, v_out)
    finish(k_in, k_out)
    attend([(own, 0)])
    k_in[4].wait_recv()
    v_in[4].wait_recv()
    take_keys(sib)
    take_values(sib)

    @pl.when(core == 1)
    def _():
        attend([(sib, 0)])

    for array in (k_in, v_in):
        for number in (7, 8):
            array[number].wait_recv()

    def pair_of(pos):
        return pos * 2 + core, pos * 2 + other_core

    def take(pos):
        for item in pair_of(pos):
            take_keys(item)
            take_values(item)

    def both(pos, side):
        return [(item, side) for item in pair_of(pos)]

    @pl.when(x >= 1)
    def _():
        take(left_x)
        attend(both(left_x, 0))

    finish(v_in, v_out)

    @pl.when(x == 3)
    def _():
        take(right_x)

    swap_queries.wait_recv()
    qt[1, :HD, :] = flat(qg[1]).T

    @pl.when(half == 0)
    def _():
        attend(both(x, 1))

    @pl.when((x == 1) | (x == 2))
    def _():
        attend(both(left_x, 1))

    @pl.when(x == 3)
    def _():
        attend(both(left_x, 1) + both(right_x, 1))

    for array in (k_in, v_in):
        for number in (9, 10):
            array[number].wait_recv()

    @pl.when(x >= 2)
    def _():
        take(far_x)
        attend(both(far_x, 1))

    total = acc[1, HD:HD + 1, :]
    part_out[...] = (acc[1, :HD, :] / jnp.where(total > 0.0, total, 1.0)).astype(BF16)
    stat_out[0:1, :] = m_buf[1]
    stat_out[1:2, :] = total
    stat_out[2:, :] = jnp.zeros((6, ROWS), F32)
    swap_part.start()
    swap_stat.start()

    @pl.when(x == 3)
    def _():
        attend(both(right_x, 0) + both(far_x, 0))

    @pl.when(x == 2)
    def _():
        attend(both(far_x, 0))

    swap_stat.wait_recv()
    swap_part.wait_recv()
    other_max, other_total = stat_in[0:1, :], stat_in[1:2, :]
    own_max, own_total = m_buf[0], acc[0, HD:HD + 1, :]
    top = jnp.maximum(own_max, other_max)
    own_scale = jnp.exp2((own_max - top) * SCALE)
    other_weight = other_total * jnp.exp2((other_max - top) * SCALE)
    denominator = own_total * own_scale + other_weight
    mixed = (acc[0, :HD, :] * own_scale + part_in[...].astype(F32) * other_weight) / denominator
    gates = gate_ref[...]
    step_id = lax.broadcasted_iota(jnp.int32, gates.shape, 0)
    gate = jnp.sum(jnp.where(step_id == step_ref[role], gates, 0.0), axis=0, keepdims=True)
    attended = mixed.T.astype(BF16).astype(F32) * gate
    obuf[...] = attended.reshape(PEERS, PIECE, HD).astype(BF16)

    def give(turn, carry):
        to_seq = source_of(turn)
        pltpu.make_async_remote_copy(
            src_ref=obuf.at[to_seq], dst_ref=out_ref.at[:, columns], send_sem=a2a_send.at[3],
            recv_sem=a2a_recv.at[3], device_id=(role, to_seq), device_id_type=MESH,
        ).start()
        return carry

    @pl.when(has_self == 1)
    def _():
        pltpu.make_async_copy(obuf.at[seq], out_ref.at[:, columns], a2a_recv.at[3]).start()

    @pl.when(has_self == 0)
    def _():
        give(0, 0)

    lax.fori_loop(1, PEERS, give, 0)

    for array in (k_out, v_out):
        for copy in array:
            copy.wait_send()
    for copy in (swap_queries, swap_part, swap_stat):
        copy.wait_send()
    whole(out_ref, a2a_recv.at[3]).wait()

    @pl.when(has_self == 1)
    def _():
        for which in range(4):
            whole(obuf.at[pl.ds(0, PEERS - 1)], a2a_send.at[which]).wait()

    @pl.when(has_self == 0)
    def _():
        for which in range(4):
            whole(obuf, a2a_send.at[which]).wait()


def shards(queries, keys, values, step_index, frame_counts, frame_layout, gate_table):
    anywhere = pl.BlockSpec(memory_space=pl.ANY)
    block = queries.shape[1:]
    piece = (PEERS, PIECE, HD)
    result = pl.pallas_call(
        kernel,
        out_shape=jax.ShapeDtypeStruct(block, BF16),
        in_specs=[anywhere] * 7,
        out_specs=pl.BlockSpec(memory_space=pltpu.VMEM),
        scratch_shapes=[
            pltpu.VMEM(block, BF16),
            pltpu.VMEM(block, BF16),
            pltpu.VMEM(block, BF16),
            pltpu.SMEM(step_index.shape, jnp.int32),
            pltpu.SMEM(frame_counts.shape, jnp.int32),
            pltpu.SMEM(frame_layout.shape, jnp.int32),
            pltpu.VMEM((gate_table.shape[0], HD), F32),
            pltpu.SemaphoreType.DMA((7,)),
            pltpu.VMEM((8, *piece), BF16),
            pltpu.VMEM((8, *piece), BF16),
            pltpu.VMEM((2, *piece), BF16),
            pltpu.VMEM((8, ROWS, 2 * HD), BF16),
            pltpu.VMEM((8, HD + 16, ROWS), BF16),
            pltpu.VMEM((2, 2 * HD, ROWS), BF16),
            pltpu.VMEM((2, ROWS, ROWS), F32),
            pltpu.VMEM((2, 1, ROWS), F32),
            pltpu.VMEM((2, HD + 16, ROWS), F32),
            pltpu.VMEM(piece, BF16),
            pltpu.VMEM((HD, ROWS), BF16),
            pltpu.VMEM((8, ROWS), F32),
            pltpu.VMEM((HD, ROWS), BF16),
            pltpu.VMEM((8, ROWS), F32),
            pltpu.SemaphoreType.DMA((4,)),
            pltpu.SemaphoreType.DMA((4,)),
            pltpu.SemaphoreType.DMA((2, 11)),
            pltpu.SemaphoreType.DMA((2, 11)),
            pltpu.SemaphoreType.DMA((3,)),
            pltpu.SemaphoreType.DMA((3,)),
        ],
        compiler_params=pltpu.CompilerParams(
            collective_id=0, has_side_effects=True, vmem_limit_bytes=60 << 20
        ),
    )(queries[0], keys[0], values[0], step_index, frame_counts, frame_layout, gate_table)
    return result[None]


def solution(mesh):
    split = P("span", "seq", None)
    return jax.shard_map(
        shards,
        mesh=mesh,
        in_specs=(split, split, split, P(), P(), P(), P()),
        out_specs=split,
        check_vma=False,
    )
```

```python
import functools
import math

import jax
import jax.numpy as jnp
from jax import lax
from jax.experimental import pallas as pl
from jax.experimental.pallas import tpu as pltpu
from jax.sharding import PartitionSpec as P

MESH = pl.DeviceIdType.MESH
HD = 128
FRAMES = 8
SPANS = 16
ROWS = 768
PIECE = 24
PEERS = 32
FRAME_ROWS = ROWS // FRAMES
SCALE = math.log2(math.e) / math.sqrt(HD)
LOW = -1e30
F32, BF16 = jnp.float32, jnp.bfloat16


def flip(plane):
    return 1 - lax.rem(lax.div(plane + 1, 2), 2)


def whole(ref, sem):
    return pltpu.make_async_copy(ref, ref, sem)


def kernel(
    q_hbm, k_hbm, v_hbm, step_hbm, count_hbm, layout_hbm, gate_hbm, out_ref,
    q_ref, k_ref, v_ref, step_ref, count_ref, layout_ref, gate_ref, load_sem, kg, vg, qg, kx, vt, qt, s_buf, m_buf, acc, obuf, part_out, stat_out, part_in, stat_in,
    a2a_send, a2a_recv, ring_send, ring_recv, pair_send, pair_recv,
):
    span = lax.axis_index("span")
    seq = lax.axis_index("seq")
    core = lax.rem(span, 2)
    z_hi = lax.rem(lax.div(span, 2), 2)
    x = lax.div(span, 4)
    z_lo = lax.div(seq, 8)
    y = lax.rem(seq, 8)
    bit = lax.rem(z_lo, 2)
    plane = z_hi * 2 + lax.div(z_lo, 2)
    half = lax.rem(bit + flip(plane), 2)
    head = plane * 8 + y
    role = (x * 2 + half) * 2 + core
    own = x * 2 + core
    has_self = (half == z_hi).astype(jnp.int32)

    def ring_span(pos):
        return (pos * 2 + z_hi) * 2 + core

    right_x, left_x, far_x = lax.rem(x + 1, 4), lax.rem(x + 3, 4), lax.rem(x + 2, 4)
    right = (ring_span(right_x), seq)
    left = (ring_span(left_x), seq)
    sibling = (span + 1 - 2 * core, seq)
    partner = (span, seq + 8 - 16 * bit)

    columns = pl.ds(pl.multiple_of(head * HD, HD), HD)
    loads = [
        pltpu.make_async_copy(source, target, load_sem.at[number])
        for number, (source, target) in enumerate((
            (k_hbm, k_ref), (v_hbm, v_ref), (q_hbm, q_ref), (count_hbm, count_ref), (layout_hbm, layout_ref),
            (step_hbm, step_ref), (gate_hbm.at[:, columns], gate_ref),
        ))
    ]
    for load in loads:
        load.start()

    barrier = pltpu.get_barrier_semaphore()

    def source_of(turn):
        return lax.rem(z_lo + lax.div(turn, 8), 4) * 8 + lax.rem(y + lax.rem(turn, 8), 8)

    def greet(turn, carry):
        pl.semaphore_signal(barrier, inc=1, device_id=(role, source_of(turn)), device_id_type=MESH)
        return carry

    lax.fori_loop(1, PEERS, greet, 0)

    @pl.when(has_self == 0)
    def _():
        greet(0, 0)

    for other in (right, left, sibling, partner):
        pl.semaphore_signal(barrier, inc=1, device_id=other, device_id_type=MESH)
    for load in loads:
        load.wait()

    def scatter(array_ref, landing, which):
        def target(turn):
            to_plane = lax.rem(plane + lax.div(turn, 8), 4)
            to_y = lax.rem(y + lax.rem(turn, 8), 8)
            to_span = (x * 2 + lax.div(to_plane, 2)) * 2 + core
            to_bit = lax.rem(flip(to_plane) + z_hi, 2)
            to_seq = (2 * lax.rem(to_plane, 2) + to_bit) * 8 + to_y
            columns = pl.ds(pl.multiple_of((to_plane * 8 + to_y) * HD, HD), HD)
            return (to_span, to_seq), array_ref.at[:, columns], landing.at[seq]

        def send(turn, carry):
            device, source, destination = target(turn)
            pltpu.make_async_remote_copy(
                src_ref=source, dst_ref=destination, send_sem=a2a_send.at[which],
                recv_sem=a2a_recv.at[which, lax.div(z_lo, 2)], device_id=device, device_id_type=MESH,
            ).start()
            return carry

        @pl.when(has_self == 1)
        def _():
            _, source, destination = target(0)
            pltpu.make_async_copy(source, destination, a2a_recv.at[which, lax.div(z_lo, 2)]).start()

        @pl.when(has_self == 0)
        def _():
            send(0, 0)

        lax.fori_loop(1, PEERS, send, 0)

    def sent(which):
        @pl.when(has_self == 1)
        def _():
            whole(obuf.at[pl.ds(0, PEERS - 1)], a2a_send.at[which]).wait()

        @pl.when(has_self == 0)
        def _():
            whole(obuf, a2a_send.at[which]).wait()

    rows = lax.broadcasted_iota(jnp.int32, (ROWS, HD), 0)
    cols = lax.broadcasted_iota(jnp.int32, (ROWS, HD), 1)
    for item in range(8):
        count = count_ref[(item // 2) * 4 + half * 2 + item % 2]
        hidden = (cols == FRAMES) & (rows >= count * FRAME_ROWS)
        kx[item, :, HD:] = jnp.where(hidden, LOW, 0.0).astype(BF16)
        vt[item, HD:, :] = jnp.ones((16, ROWS), BF16)
    first = cols * FRAME_ROWS
    kx[own, :, HD:] = ((cols < FRAMES) & (rows >= first) & (rows < first + FRAME_ROWS)).astype(F32).astype(BF16)
    frame_id = lax.broadcasted_iota(jnp.int32, (16, ROWS), 0)
    lane = lax.broadcasted_iota(jnp.int32, (16, ROWS), 1)
    own_count = count_ref[role]
    hit = jnp.zeros((16, ROWS), jnp.int32)
    for q_frame in range(FRAMES):
        column = jnp.zeros((16, ROWS), jnp.int32)
        for k_frame in range(FRAMES):
            column = jnp.where(frame_id == k_frame, layout_ref[q_frame, k_frame], column)
        inside = (lane >= q_frame * FRAME_ROWS) & (lane < (q_frame + 1) * FRAME_ROWS)
        hit = jnp.where(inside, column, hit)
    valid = frame_id < own_count
    same = (lane >= frame_id * FRAME_ROWS) & (lane < (frame_id + 1) * FRAME_ROWS)
    shown = (valid & (hit == 1)) | same
    one_row = jnp.where(frame_id == FRAMES, 1.0, 0.0)
    in_frames = frame_id < FRAMES
    qt[0, HD:HD + 16, :] = jnp.where(in_frames & jnp.logical_not(shown), LOW, one_row).astype(BF16)
    qt[1, HD:HD + 16, :] = jnp.where(in_frames & jnp.logical_not(valid), LOW, one_row).astype(BF16)
    qt[:, HD + 16:, :] = jnp.zeros((2, HD - 16, ROWS), BF16)
    m_buf[...] = jnp.full_like(m_buf, LOW)
    acc[...] = jnp.zeros_like(acc)

    pl.semaphore_wait(barrier, PEERS + 4 - has_self)

    gathered = (kg, vg)

    def hop(array, number, item, device, rows_from=0, row_count=PEERS):
        piece = gathered[array].at[item, pl.ds(rows_from, row_count)]
        return pltpu.make_async_remote_copy(
            src_ref=piece, dst_ref=piece, send_sem=ring_send.at[array, number],
            recv_sem=ring_recv.at[array, number], device_id=device, device_id_type=MESH,
        )

    other_core = 1 - core
    left_item, right_item, far_item = left_x * 2 + core, right_x * 2 + core, far_x * 2 + core
    late = (plane == 2 * half).astype(jnp.int32)
    early = 1 - late
    lower, upper = (early * (PEERS // 2), PEERS // 2), (late * (PEERS // 2), PEERS // 2)

    def arrived(array_ref, which, part):
        whole(array_ref.at[pl.ds(part * (PEERS // 2), PEERS // 2)], a2a_recv.at[which, part]).wait()

    def outgoing(array):
        return (
            hop(array, 0, own, right, *lower),
            hop(array, 1, own, right, *upper),
            hop(array, 2, own, left, *upper),
            hop(array, 3, own, left, *lower),
            hop(array, 4, own, sibling),
            hop(array, 5, left_item, right, *lower),
            hop(array, 6, right_item, left, *upper),
            hop(array, 7, left_item, sibling),
            hop(array, 8, right_item, sibling),
            hop(array, 9, far_item, sibling, *lower),
            hop(array, 10, far_item, sibling, *upper),
        )

    def incoming(array):
        return (
            hop(array, 0, left_item, right, *lower),
            hop(array, 1, left_item, right, *upper),
            hop(array, 2, right_item, left, *upper),
            hop(array, 3, right_item, left, *lower),
            hop(array, 4, x * 2 + other_core, sibling),
            hop(array, 5, far_item, right, *lower),
            hop(array, 6, far_item, left, *upper),
            hop(array, 7, left_x * 2 + other_core, sibling),
            hop(array, 8, right_x * 2 + other_core, sibling),
            hop(array, 9, far_x * 2 + other_core, sibling, *lower),
            hop(array, 10, far_x * 2 + other_core, sibling, *upper),
        )

    k_out, v_out, k_in, v_in = outgoing(0), outgoing(1), incoming(0), incoming(1)

    def flat(piece):
        return piece.astype(F32).reshape(ROWS, HD).astype(BF16)

    def take_keys(item):
        kx[item, :, :HD] = flat(kg[item])

    def take_values(item):
        vt[item, :HD, :] = flat(vg[item]).T

    def scores(slot, item, side):
        result = jnp.dot(kx[item], qt[side], preferred_element_type=F32)
        s_buf[slot] = result
        return jnp.max(result, axis=0, keepdims=True)

    def absorb(slot, item, side, block_max):
        old_max = m_buf[side]
        new_max = jnp.maximum(old_max, block_max)
        weights = jnp.exp2(s_buf[slot] * SCALE - new_max * SCALE).astype(BF16)
        summed = jnp.dot(vt[item], weights, preferred_element_type=F32)
        acc[side] = acc[side] * jnp.exp2((old_max - new_max) * SCALE) + summed
        m_buf[side] = new_max

    def attend(blocks):
        block_max = scores(0, *blocks[0])
        for number, block in enumerate(blocks):
            if number + 1 < len(blocks):
                next_max = scores((number + 1) % 2, *blocks[number + 1])
            absorb(number % 2, *block, block_max)
            if number + 1 < len(blocks):
                block_max = next_max

    def pair(ref_out, ref_in, number):
        return pltpu.make_async_remote_copy(
            src_ref=ref_out, dst_ref=ref_in, send_sem=pair_send.at[number],
            recv_sem=pair_recv.at[number], device_id=partner, device_id_type=MESH,
        )

    swap_early = pair(qg.at[0, pl.ds(*lower)], qg.at[1, pl.ds(*lower)], 0)
    swap_late = pair(qg.at[0, pl.ds(*upper)], qg.at[1, pl.ds(*upper)], 1)
    half_rows = (pl.ds(0, ROWS // 2), pl.ds(ROWS // 2, ROWS // 2))
    swap_parts = [pair(part_out.at[:, at], part_in.at[:, at], 2 + number) for number, at in enumerate(half_rows)]
    swap_stat = pair(stat_out, stat_in, 4)

    sib = x * 2 + other_core

    last = x == 3
    sends_own, has_left_item, has_right_item, has_far_item = x != 3, x != 0, x != 2, x != 1
    always = x >= 0
    needed = (sends_own,) * 4 + (always, has_left_item, has_right_item, has_left_item, has_right_item, has_far_item, has_far_item)
    expected = (has_left_item,) * 2 + (has_right_item,) * 2 + (always, has_far_item, has_far_item) + needed[7:]

    def start(copies, *numbers):
        for number in numbers:
            pl.when(needed[number])(copies[number].start)

    def wait(copies, *numbers):
        for number in numbers:
            pl.when(expected[number])(copies[number].wait_recv)

    def begin(array, which, copies):
        arrived(array.at[own], which, early)
        start(copies, 0, 3)
        arrived(array.at[own], which, late)
        start(copies, 2, 1, 4)

    def relay(arriving, leaving):
        wait(arriving, 0)
        start(leaving, 5)
        wait(arriving, 3, 2)
        start(leaving, 6, 8)
        wait(arriving, 1)
        start(leaving, 7)

    def finish(arriving, leaving):
        for number in (5, 6):
            wait(arriving, number)
            start(leaving, number + 4)

    def exchange_queries():
        for part, swap in ((early, swap_early), (late, swap_late)):
            arrived(qg.at[0], 0, part)
            swap.start()

    @pl.when(last)
    def _():
        scatter(q_ref, qg.at[0], 0)
        sent(0)
        scatter(k_ref, kg.at[own], 1)
        exchange_queries()
        sent(1)
        scatter(v_ref, vg.at[own], 2)

    @pl.when(sends_own)
    def _():
        scatter(k_ref, kg.at[own], 1)
        sent(1)
        scatter(v_ref, vg.at[own], 2)

    begin(kg, 1, k_out)

    @pl.when(sends_own)
    def _():
        sent(2)
        scatter(q_ref, qg.at[0], 0)

    take_keys(own)

    @pl.when(last)
    def _():
        relay(k_in, k_out)

    begin(vg, 2, v_out)
    take_values(own)

    @pl.when(sends_own)
    def _():
        relay(k_in, k_out)
        exchange_queries()

    qt[0, :HD, :] = flat(qg[0]).T
    relay(v_in, v_out)
    finish(k_in, k_out)
    attend([(own, 0)])
    k_in[4].wait_recv()
    v_in[4].wait_recv()
    take_keys(sib)
    take_values(sib)

    @pl.when(core == 1)
    def _():
        attend([(sib, 0)])

    for array in (k_in, v_in):
        wait(array, 7, 8)

    def pair_of(pos):
        return pos * 2 + core, pos * 2 + other_core

    def take(pos):
        for item in pair_of(pos):
            take_keys(item)
            take_values(item)

    @pl.when(x >= 1)
    def _():
        take(left_x)

    def send_part():
        total = acc[1, HD:HD + 1, :]
        stat_out[0:1, :] = m_buf[1]
        stat_out[1:2, :] = total
        stat_out[2:, :] = jnp.zeros((6, ROWS), F32)
        swap_stat.start()
        part_out[...] = (acc[1, :HD, :] / jnp.where(total > 0.0, total, 1.0)).astype(BF16)
        for swap in swap_parts:
            swap.start()

    def open_phase(phase):
        @pl.when(phase == 1)
        def _():
            finish(v_in, v_out)

            @pl.when(x == 3)
            def _():
                take(right_x)

            swap_early.wait_recv()
            swap_late.wait_recv()
            qt[1, :HD, :] = flat(qg[1]).T

        @pl.when(phase == 2)
        def _():
            for array in (k_in, v_in):
                wait(array, 9, 10)

            @pl.when(x >= 2)
            def _():
                take(far_x)

        @pl.when(phase == 3)
        def _():
            send_part()

    has_left, has_right, has_far = ((x >= 1).astype(jnp.int32), (x == 3).astype(jnp.int32), (x >= 2).astype(jnp.int32))

    def run_phase(phase, carry):
        open_phase(phase)
        side = ((phase == 1) | (phase == 2)).astype(jnp.int32)
        skip = jnp.where(phase == 0, 1, jnp.where(phase == 1, half, jnp.where(phase == 2, 3, 3 - has_right)))
        stop = jnp.where(phase == 0, 1 + has_left, jnp.where(phase == 1, 1 + has_left + has_right, 3 + has_far))

        def run_pair(turn, inner):
            pos = jnp.where(turn == 0, x, jnp.where(turn == 1, left_x, jnp.where(turn == 2, right_x, far_x)))
            attend([(pos * 2 + core, side), (pos * 2 + other_core, side)])
            return inner

        return lax.fori_loop(skip, stop, run_pair, carry)

    lax.fori_loop(0, 4, run_phase, 0)
    gates = gate_ref[...]
    step_id = lax.broadcasted_iota(jnp.int32, gates.shape, 0)
    gate = jnp.sum(jnp.where(step_id == step_ref[role], gates, 0.0), axis=0, keepdims=True)
    swap_stat.wait_recv()

    def give(turn, part):
        to_seq = lax.rem(part * 2 + lax.rem(lax.div(turn, 8) + z_lo, 2), 4) * 8 + lax.rem(y + lax.rem(turn, 8), 8)
        here = (role == span) & (to_seq == seq)

        @pl.when(here)
        def _():
            pltpu.make_async_copy(obuf.at[to_seq], out_ref.at[:, columns], a2a_recv.at[3, 0]).start()

        @pl.when(jnp.logical_not(here))
        def _():
            pltpu.make_async_remote_copy(
                src_ref=obuf.at[to_seq], dst_ref=out_ref.at[:, columns], send_sem=a2a_send.at[3],
                recv_sem=a2a_recv.at[3, 0], device_id=(role, to_seq), device_id_type=MESH,
            ).start()

        return part

    for part in range(2):
        at = slice(part * (ROWS // 2), (part + 1) * (ROWS // 2))
        swap_parts[part].wait_recv()
        other_max, other_total = stat_in[0:1, at], stat_in[1:2, at]
        own_max, own_total = m_buf[0, :, at], acc[0, HD:HD + 1, at]
        top = jnp.maximum(own_max, other_max)
        own_scale = jnp.exp2((own_max - top) * SCALE)
        other_weight = other_total * jnp.exp2((other_max - top) * SCALE)
        denominator = own_total * own_scale + other_weight
        mixed = (acc[0, :HD, at] * own_scale + part_in[:, at].astype(F32) * other_weight) / denominator
        attended = mixed.T.astype(BF16).astype(F32) * gate
        obuf[part * (PEERS // 2):(part + 1) * (PEERS // 2)] = attended.reshape(PEERS // 2, PIECE, HD).astype(BF16)
        lax.fori_loop(0, PEERS // 2, give, part)

    for array in (k_out, v_out):
        for number, copy in enumerate(array):
            pl.when(needed[number])(copy.wait_send)
    for copy in (swap_early, swap_late, *swap_parts, swap_stat):
        copy.wait_send()
    whole(out_ref, a2a_recv.at[3, 0]).wait()
    pl.when(last)(lambda: sent(2))
    pl.when(sends_own)(lambda: sent(0))
    sent(3)


def shards(queries, keys, values, step_index, frame_counts, frame_layout, gate_table):
    anywhere = pl.BlockSpec(memory_space=pl.ANY)
    block = queries.shape[1:]
    piece = (PEERS, PIECE, HD)
    result = pl.pallas_call(
        kernel,
        out_shape=jax.ShapeDtypeStruct(block, BF16),
        in_specs=[anywhere] * 7,
        out_specs=pl.BlockSpec(memory_space=pltpu.VMEM),
        scratch_shapes=[
            pltpu.VMEM(block, BF16),
            pltpu.VMEM(block, BF16),
            pltpu.VMEM(block, BF16),
            pltpu.SMEM(step_index.shape, jnp.int32),
            pltpu.SMEM(frame_counts.shape, jnp.int32),
            pltpu.SMEM(frame_layout.shape, jnp.int32),
            pltpu.VMEM((gate_table.shape[0], HD), F32),
            pltpu.SemaphoreType.DMA((7,)),
            pltpu.VMEM((8, *piece), BF16),
            pltpu.VMEM((8, *piece), BF16),
            pltpu.VMEM((2, *piece), BF16),
            pltpu.VMEM((8, ROWS, 2 * HD), BF16),
            pltpu.VMEM((8, HD + 16, ROWS), BF16),
            pltpu.VMEM((2, 2 * HD, ROWS), BF16),
            pltpu.VMEM((2, ROWS, ROWS), F32),
            pltpu.VMEM((2, 1, ROWS), F32),
            pltpu.VMEM((2, HD + 16, ROWS), F32),
            pltpu.VMEM(piece, BF16),
            pltpu.VMEM((HD, ROWS), BF16),
            pltpu.VMEM((8, ROWS), F32),
            pltpu.VMEM((HD, ROWS), BF16),
            pltpu.VMEM((8, ROWS), F32),
            pltpu.SemaphoreType.DMA((4,)),
            pltpu.SemaphoreType.DMA((4, 2)),
            pltpu.SemaphoreType.DMA((2, 11)),
            pltpu.SemaphoreType.DMA((2, 11)),
            pltpu.SemaphoreType.DMA((5,)),
            pltpu.SemaphoreType.DMA((5,)),
        ],
        compiler_params=pltpu.CompilerParams(
            collective_id=0, has_side_effects=True, vmem_limit_bytes=60 << 20
        ),
    )(queries[0], keys[0], values[0], step_index, frame_counts, frame_layout, gate_table)
    return result[None]


def solution(mesh):
    split = P("span", "seq", None)
    return jax.shard_map(
        shards,
        mesh=mesh,
        in_specs=(split, split, split, P(), P(), P(), P()),
        out_specs=split,
        check_vma=False,
    )
```

```python
import functools
import math

import jax
import jax.numpy as jnp
from jax import lax
from jax.experimental import pallas as pl
from jax.experimental.pallas import tpu as pltpu
from jax.sharding import PartitionSpec as P

MESH = pl.DeviceIdType.MESH
HD = 128
FRAMES = 8
SPANS = 16
ROWS = 768
PIECE = 24
PEERS = 32
FRAME_ROWS = ROWS // FRAMES
SCALE = math.log2(math.e) / math.sqrt(HD)
LOW = -1e30
F32, BF16 = jnp.float32, jnp.bfloat16


def flip(plane):
    return 1 - lax.rem(lax.div(plane + 1, 2), 2)


def whole(ref, sem):
    return pltpu.make_async_copy(ref, ref, sem)


def kernel(
    q_hbm, k_hbm, v_hbm, step_hbm, count_hbm, layout_hbm, gate_hbm, out_ref,
    q_ref, k_ref, v_ref, step_ref, count_ref, layout_ref, gate_ref, load_sem, kg, vg, qg, kx, vt, qt, s_buf, m_buf, acc, obuf, part_out, stat_out, part_in, stat_in,
    a2a_send, a2a_recv, ring_send, ring_recv, pair_send, pair_recv,
):
    span = lax.axis_index("span")
    seq = lax.axis_index("seq")
    core = lax.rem(span, 2)
    z_hi = lax.rem(lax.div(span, 2), 2)
    x = lax.div(span, 4)
    z_lo = lax.div(seq, 8)
    y = lax.rem(seq, 8)
    bit = lax.rem(z_lo, 2)
    plane = z_hi * 2 + lax.div(z_lo, 2)
    half = lax.rem(bit + flip(plane), 2)
    head = plane * 8 + y
    role = (x * 2 + half) * 2 + core
    own = x * 2 + core
    has_self = (half == z_hi).astype(jnp.int32)

    def ring_span(pos):
        return (pos * 2 + z_hi) * 2 + core

    right_x, left_x, far_x = lax.rem(x + 1, 4), lax.rem(x + 3, 4), lax.rem(x + 2, 4)
    right = (ring_span(right_x), seq)
    left = (ring_span(left_x), seq)
    sibling = (span + 1 - 2 * core, seq)
    partner = (span, seq + 8 - 16 * bit)

    columns = pl.ds(pl.multiple_of(head * HD, HD), HD)
    loads = [
        pltpu.make_async_copy(source, target, load_sem.at[number])
        for number, (source, target) in enumerate((
            (k_hbm, k_ref), (v_hbm, v_ref), (q_hbm, q_ref), (count_hbm, count_ref), (layout_hbm, layout_ref),
            (step_hbm, step_ref), (gate_hbm.at[:, columns], gate_ref),
        ))
    ]
    for load in loads:
        load.start()

    barrier = pltpu.get_barrier_semaphore()

    def source_of(turn):
        return lax.rem(z_lo + lax.div(turn, 8), 4) * 8 + lax.rem(y + lax.rem(turn, 8), 8)

    def greet(turn, carry):
        pl.semaphore_signal(barrier, inc=1, device_id=(role, source_of(turn)), device_id_type=MESH)
        return carry

    lax.fori_loop(1, PEERS, greet, 0)

    @pl.when(has_self == 0)
    def _():
        greet(0, 0)

    for other in (right, left, sibling, partner):
        pl.semaphore_signal(barrier, inc=1, device_id=other, device_id_type=MESH)
    for load in loads:
        load.wait()

    def scatter(array_ref, landing, which):
        def target(turn):
            to_plane = lax.rem(plane + lax.div(turn, 8), 4)
            to_y = lax.rem(y + lax.rem(turn, 8), 8)
            to_span = (x * 2 + lax.div(to_plane, 2)) * 2 + core
            to_bit = lax.rem(flip(to_plane) + z_hi, 2)
            to_seq = (2 * lax.rem(to_plane, 2) + to_bit) * 8 + to_y
            columns = pl.ds(pl.multiple_of((to_plane * 8 + to_y) * HD, HD), HD)
            return (to_span, to_seq), array_ref.at[:, columns], landing.at[seq]

        def send(turn, carry):
            device, source, destination = target(turn)
            pltpu.make_async_remote_copy(
                src_ref=source, dst_ref=destination, send_sem=a2a_send.at[which],
                recv_sem=a2a_recv.at[which, lax.div(z_lo, 2)], device_id=device, device_id_type=MESH,
            ).start()
            return carry

        @pl.when(has_self == 1)
        def _():
            _, source, destination = target(0)
            pltpu.make_async_copy(source, destination, a2a_recv.at[which, lax.div(z_lo, 2)]).start()

        @pl.when(has_self == 0)
        def _():
            send(0, 0)

        lax.fori_loop(1, PEERS, send, 0)

    def sent(which):
        @pl.when(has_self == 1)
        def _():
            whole(obuf.at[pl.ds(0, PEERS - 1)], a2a_send.at[which]).wait()

        @pl.when(has_self == 0)
        def _():
            whole(obuf, a2a_send.at[which]).wait()

    rows = lax.broadcasted_iota(jnp.int32, (ROWS, HD), 0)
    cols = lax.broadcasted_iota(jnp.int32, (ROWS, HD), 1)
    for item in range(8):
        count = count_ref[(item // 2) * 4 + half * 2 + item % 2]
        hidden = (cols == FRAMES) & (rows >= count * FRAME_ROWS)
        kx[item, :, HD:] = jnp.where(hidden, LOW, 0.0).astype(BF16)
        vt[item, HD:, :] = jnp.ones((16, ROWS), BF16)
    first = cols * FRAME_ROWS
    kx[own, :, HD:] = ((cols < FRAMES) & (rows >= first) & (rows < first + FRAME_ROWS)).astype(F32).astype(BF16)
    frame_id = lax.broadcasted_iota(jnp.int32, (16, ROWS), 0)
    lane = lax.broadcasted_iota(jnp.int32, (16, ROWS), 1)
    own_count = count_ref[role]
    hit = jnp.zeros((16, ROWS), jnp.int32)
    for q_frame in range(FRAMES):
        column = jnp.zeros((16, ROWS), jnp.int32)
        for k_frame in range(FRAMES):
            column = jnp.where(frame_id == k_frame, layout_ref[q_frame, k_frame], column)
        inside = (lane >= q_frame * FRAME_ROWS) & (lane < (q_frame + 1) * FRAME_ROWS)
        hit = jnp.where(inside, column, hit)
    valid = frame_id < own_count
    same = (lane >= frame_id * FRAME_ROWS) & (lane < (frame_id + 1) * FRAME_ROWS)
    shown = (valid & (hit == 1)) | same
    one_row = jnp.where(frame_id == FRAMES, 1.0, 0.0)
    in_frames = frame_id < FRAMES
    qt[0, HD:HD + 16, :] = jnp.where(in_frames & jnp.logical_not(shown), LOW, one_row).astype(BF16)
    qt[1, HD:HD + 16, :] = jnp.where(in_frames & jnp.logical_not(valid), LOW, one_row).astype(BF16)
    qt[:, HD + 16:, :] = jnp.zeros((2, HD - 16, ROWS), BF16)
    m_buf[...] = jnp.full_like(m_buf, LOW)
    acc[...] = jnp.zeros_like(acc)

    pl.semaphore_wait(barrier, PEERS + 4 - has_self)

    gathered = (kg, vg)

    def hop(array, number, item, device, rows_from=0, row_count=PEERS):
        piece = gathered[array].at[item, pl.ds(rows_from, row_count)]
        return pltpu.make_async_remote_copy(
            src_ref=piece, dst_ref=piece, send_sem=ring_send.at[array, number],
            recv_sem=ring_recv.at[array, number], device_id=device, device_id_type=MESH,
        )

    other_core = 1 - core
    left_item, right_item, far_item = left_x * 2 + core, right_x * 2 + core, far_x * 2 + core
    late = (plane == 2 * half).astype(jnp.int32)
    early = 1 - late
    lower, upper = (early * (PEERS // 2), PEERS // 2), (late * (PEERS // 2), PEERS // 2)

    def arrived(array_ref, which, part):
        whole(array_ref.at[pl.ds(part * (PEERS // 2), PEERS // 2)], a2a_recv.at[which, part]).wait()

    def outgoing(array):
        return (
            hop(array, 0, own, right, *lower),
            hop(array, 1, own, right, *upper),
            hop(array, 2, own, left, *upper),
            hop(array, 3, own, left, *lower),
            hop(array, 4, own, sibling),
            hop(array, 5, left_item, right, *lower),
            hop(array, 6, right_item, left, *upper),
            hop(array, 7, left_item, sibling),
            hop(array, 8, right_item, sibling),
            hop(array, 9, far_item, sibling, *lower),
            hop(array, 10, far_item, sibling, *upper),
        )

    def incoming(array):
        return (
            hop(array, 0, left_item, right, *lower),
            hop(array, 1, left_item, right, *upper),
            hop(array, 2, right_item, left, *upper),
            hop(array, 3, right_item, left, *lower),
            hop(array, 4, x * 2 + other_core, sibling),
            hop(array, 5, far_item, right, *lower),
            hop(array, 6, far_item, left, *upper),
            hop(array, 7, left_x * 2 + other_core, sibling),
            hop(array, 8, right_x * 2 + other_core, sibling),
            hop(array, 9, far_x * 2 + other_core, sibling, *lower),
            hop(array, 10, far_x * 2 + other_core, sibling, *upper),
        )

    k_out, v_out, k_in, v_in = outgoing(0), outgoing(1), incoming(0), incoming(1)

    def flat(piece):
        return piece.astype(F32).reshape(ROWS, HD).astype(BF16)

    def take_keys(item):
        kx[item, :, :HD] = flat(kg[item])

    def take_values(item):
        vt[item, :HD, :] = flat(vg[item]).T

    def scores(slot, item, side):
        result = jnp.dot(kx[item], qt[side], preferred_element_type=F32)
        s_buf[slot] = result
        return jnp.max(result, axis=0, keepdims=True)

    def absorb(slot, item, side, block_max):
        old_max = m_buf[side]
        new_max = jnp.maximum(old_max, block_max)
        weights = jnp.exp2(s_buf[slot] * SCALE - new_max * SCALE).astype(BF16)
        summed = jnp.dot(vt[item], weights, preferred_element_type=F32)
        acc[side] = acc[side] * jnp.exp2((old_max - new_max) * SCALE) + summed
        m_buf[side] = new_max

    def attend(blocks):
        block_max = scores(0, *blocks[0])
        for number, block in enumerate(blocks):
            if number + 1 < len(blocks):
                next_max = scores((number + 1) % 2, *blocks[number + 1])
            absorb(number % 2, *block, block_max)
            if number + 1 < len(blocks):
                block_max = next_max

    def pair(ref_out, ref_in, number):
        return pltpu.make_async_remote_copy(
            src_ref=ref_out, dst_ref=ref_in, send_sem=pair_send.at[number],
            recv_sem=pair_recv.at[number], device_id=partner, device_id_type=MESH,
        )

    swap_early = pair(qg.at[0, pl.ds(*lower)], qg.at[1, pl.ds(*lower)], 0)
    swap_late = pair(qg.at[0, pl.ds(*upper)], qg.at[1, pl.ds(*upper)], 1)
    half_rows = (pl.ds(0, ROWS // 2), pl.ds(ROWS // 2, ROWS // 2))
    swap_parts = [pair(part_out.at[:, at], part_in.at[:, at], 2 + number) for number, at in enumerate(half_rows)]
    swap_stat = pair(stat_out, stat_in, 4)

    sib = x * 2 + other_core

    last = x == 3
    sends_own = x != 3
    always = x >= 0
    ends, middle, later = (x == 0) | last, (x == 1) | (x == 2), x >= 2
    needed = (sends_own, sends_own, x <= 1, x == 0, always, middle, ends, x >= 1, last, later, later)
    expected = (x >= 1, x >= 1, ends, last, always, later, later, x >= 1, last, later, later)

    def start(copies, *numbers):
        for number in numbers:
            pl.when(needed[number])(copies[number].start)

    def wait(copies, *numbers):
        for number in numbers:
            pl.when(expected[number])(copies[number].wait_recv)

    def begin(array, which, copies):
        arrived(array.at[own], which, early)
        start(copies, 0, 3)
        arrived(array.at[own], which, late)
        start(copies, 2, 1, 4)

    def relay(arriving, leaving):
        wait(arriving, 0)
        start(leaving, 5)
        wait(arriving, 3, 2)
        start(leaving, 6, 8)
        wait(arriving, 1)
        start(leaving, 7)

    def finish(arriving, leaving):
        for number in (5, 6):
            wait(arriving, number)
            start(leaving, number + 4)

    def exchange_queries():
        for part, swap in ((early, swap_early), (late, swap_late)):
            arrived(qg.at[0], 0, part)
            swap.start()

    @pl.when(last)
    def _():
        scatter(q_ref, qg.at[0], 0)
        sent(0)
        scatter(k_ref, kg.at[own], 1)
        exchange_queries()
        sent(1)
        scatter(v_ref, vg.at[own], 2)

    @pl.when(sends_own)
    def _():
        scatter(k_ref, kg.at[own], 1)
        sent(1)
        scatter(v_ref, vg.at[own], 2)

    begin(kg, 1, k_out)

    @pl.when(sends_own)
    def _():
        sent(2)
        scatter(q_ref, qg.at[0], 0)

    take_keys(own)

    @pl.when(last)
    def _():
        relay(k_in, k_out)

    begin(vg, 2, v_out)
    take_values(own)

    @pl.when(sends_own)
    def _():
        relay(k_in, k_out)
        exchange_queries()

    qt[0, :HD, :] = flat(qg[0]).T
    relay(v_in, v_out)
    finish(k_in, k_out)
    attend([(own, 0)])
    k_in[4].wait_recv()
    v_in[4].wait_recv()
    take_keys(sib)
    take_values(sib)

    @pl.when(core == 1)
    def _():
        attend([(sib, 0)])

    for array in (k_in, v_in):
        wait(array, 7, 8)

    def pair_of(pos):
        return pos * 2 + core, pos * 2 + other_core

    def take(pos):
        for item in pair_of(pos):
            take_keys(item)
            take_values(item)

    @pl.when(x >= 1)
    def _():
        take(left_x)

    def send_part():
        total = acc[1, HD:HD + 1, :]
        stat_out[0:1, :] = m_buf[1]
        stat_out[1:2, :] = total
        stat_out[2:, :] = jnp.zeros((6, ROWS), F32)
        swap_stat.start()
        part_out[...] = (acc[1, :HD, :] / jnp.where(total > 0.0, total, 1.0)).astype(BF16)
        for swap in swap_parts:
            swap.start()

    def both(pos, side):
        return [(pos * 2 + core, side), (pos * 2 + other_core, side)]

    @pl.when(x >= 1)
    def _():
        attend(both(left_x, 0))

    finish(v_in, v_out)
    pl.when(last)(lambda: take(right_x))
    swap_early.wait_recv()
    swap_late.wait_recv()
    qt[1, :HD, :] = flat(qg[1]).T
    pl.when(half == 0)(lambda: attend(both(x, 1)))
    pl.when(middle)(lambda: attend(both(left_x, 1)))
    pl.when(last)(lambda: attend(both(left_x, 1) + both(right_x, 1)))
    for array in (k_in, v_in):
        wait(array, 9, 10)

    @pl.when(later)
    def _():
        take(far_x)
        attend(both(far_x, 1))

    send_part()
    pl.when(last)(lambda: attend(both(right_x, 0) + both(far_x, 0)))
    pl.when(x == 2)(lambda: attend(both(far_x, 0)))

    gates = gate_ref[...]
    step_id = lax.broadcasted_iota(jnp.int32, gates.shape, 0)
    gate = jnp.sum(jnp.where(step_id == step_ref[role], gates, 0.0), axis=0, keepdims=True)
    swap_stat.wait_recv()

    def give(turn, part):
        to_seq = lax.rem(part * 2 + lax.rem(lax.div(turn, 8) + z_lo, 2), 4) * 8 + lax.rem(y + lax.rem(turn, 8), 8)
        here = (role == span) & (to_seq == seq)

        @pl.when(here)
        def _():
            pltpu.make_async_copy(obuf.at[to_seq], out_ref.at[:, columns], a2a_recv.at[3, 0]).start()

        @pl.when(jnp.logical_not(here))
        def _():
            pltpu.make_async_remote_copy(
                src_ref=obuf.at[to_seq], dst_ref=out_ref.at[:, columns], send_sem=a2a_send.at[3],
                recv_sem=a2a_recv.at[3, 0], device_id=(role, to_seq), device_id_type=MESH,
            ).start()

        return part

    for part in range(2):
        at = slice(part * (ROWS // 2), (part + 1) * (ROWS // 2))
        swap_parts[part].wait_recv()
        other_max, other_total = stat_in[0:1, at], stat_in[1:2, at]
        own_max, own_total = m_buf[0, :, at], acc[0, HD:HD + 1, at]
        top = jnp.maximum(own_max, other_max)
        own_scale = jnp.exp2((own_max - top) * SCALE)
        other_weight = other_total * jnp.exp2((other_max - top) * SCALE)
        denominator = own_total * own_scale + other_weight
        mixed = (acc[0, :HD, at] * own_scale + part_in[:, at].astype(F32) * other_weight) / denominator
        attended = mixed.T.astype(BF16).astype(F32) * gate
        obuf[part * (PEERS // 2):(part + 1) * (PEERS // 2)] = attended.reshape(PEERS // 2, PIECE, HD).astype(BF16)
        lax.fori_loop(0, PEERS // 2, give, part)

    for array in (k_out, v_out):
        for number, copy in enumerate(array):
            pl.when(needed[number])(copy.wait_send)
    for copy in (swap_early, swap_late, *swap_parts, swap_stat):
        copy.wait_send()
    whole(out_ref, a2a_recv.at[3, 0]).wait()
    pl.when(last)(lambda: sent(2))
    pl.when(sends_own)(lambda: sent(0))
    sent(3)


def shards(queries, keys, values, step_index, frame_counts, frame_layout, gate_table):
    anywhere = pl.BlockSpec(memory_space=pl.ANY)
    block = queries.shape[1:]
    piece = (PEERS, PIECE, HD)
    result = pl.pallas_call(
        kernel,
        out_shape=jax.ShapeDtypeStruct(block, BF16),
        in_specs=[anywhere] * 7,
        out_specs=pl.BlockSpec(memory_space=pltpu.VMEM),
        scratch_shapes=[
            pltpu.VMEM(block, BF16),
            pltpu.VMEM(block, BF16),
            pltpu.VMEM(block, BF16),
            pltpu.SMEM(step_index.shape, jnp.int32),
            pltpu.SMEM(frame_counts.shape, jnp.int32),
            pltpu.SMEM(frame_layout.shape, jnp.int32),
            pltpu.VMEM((gate_table.shape[0], HD), F32),
            pltpu.SemaphoreType.DMA((7,)),
            pltpu.VMEM((8, *piece), BF16),
            pltpu.VMEM((8, *piece), BF16),
            pltpu.VMEM((2, *piece), BF16),
            pltpu.VMEM((8, ROWS, 2 * HD), BF16),
            pltpu.VMEM((8, HD + 16, ROWS), BF16),
            pltpu.VMEM((2, 2 * HD, ROWS), BF16),
            pltpu.VMEM((2, ROWS, ROWS), F32),
            pltpu.VMEM((2, 1, ROWS), F32),
            pltpu.VMEM((2, HD + 16, ROWS), F32),
            pltpu.VMEM(piece, BF16),
            pltpu.VMEM((HD, ROWS), BF16),
            pltpu.VMEM((8, ROWS), F32),
            pltpu.VMEM((HD, ROWS), BF16),
            pltpu.VMEM((8, ROWS), F32),
            pltpu.SemaphoreType.DMA((4,)),
            pltpu.SemaphoreType.DMA((4, 2)),
            pltpu.SemaphoreType.DMA((2, 11)),
            pltpu.SemaphoreType.DMA((2, 11)),
            pltpu.SemaphoreType.DMA((5,)),
            pltpu.SemaphoreType.DMA((5,)),
        ],
        compiler_params=pltpu.CompilerParams(
            collective_id=0, has_side_effects=True, vmem_limit_bytes=60 << 20
        ),
    )(queries[0], keys[0], values[0], step_index, frame_counts, frame_layout, gate_table)
    return result[None]


def solution(mesh):
    split = P("span", "seq", None)
    return jax.shard_map(
        shards,
        mesh=mesh,
        in_specs=(split, split, split, P(), P(), P(), P()),
        out_specs=split,
        check_vma=False,
    )
```
